256 devices in a mesh: snode: 64 (over x, z, core), rows: 4 (over y).
Axes of the slice: x: 4, y: 4, z: 8, core: 2. Of those that a mesh axis runs over, the one named last changes fastest.
Arguments:
- root_covariance: bfloat16 [4096, 4096], P('rows'), may hold values from -6 to 6
- ancestors: int32 [64, 4], replicated, may hold values from 0 to 7, as said below
- parents: int32 [64], replicated, may hold values from 0 to 63
- panel_first: bfloat16 [64, 2048, 512], P('snode', 'rows'), may hold values from -0.125 to 0.125
- inverse_first: bfloat16 [64, 512, 512], P('snode', 'rows'), may hold values from -6 to 6
- panel_upper: bfloat16 [64, 512, 512], P('snode', 'rows'), may hold values from -0.125 to 0.125
- panel_lower: bfloat16 [64, 2048, 512], P('snode', 'rows'), may hold values from -0.125 to 0.125
- inverse_second: bfloat16 [64, 512, 512], P('snode', 'rows'), may hold values from -6 to 6
Outputs:
- offdiag_first: bfloat16 [64, 2048, 512], P('snode', 'rows')
- diagonal_first: bfloat16 [64, 512, 512], P('snode', 'rows')
- offdiag_upper: bfloat16 [64, 512, 512], P('snode', 'rows')
- offdiag_lower: bfloat16 [64, 2048, 512], P('snode', 'rows')
- diagonal_second: bfloat16 [64, 512, 512], P('snode', 'rows')
The draws below stay inside these ranges and needn't reach their ends.
Inputs may be any that keep to these rules, and one draw needn't show every extreme that they name: `ancestors`: each row holds 4 different root block numbers.
All inputs are finite; a program needn't handle non-finite values.
Results may differ from the reference program's by a relative error of at most 0.018.
Values may be sent and summed in bfloat16 or wider, within the bound.
No kernel may reach another device: no remote copies, remote signals or barrier semaphores. Data moves between devices by JAX's collectives and lax.ppermute only.
A program may use at most 128 MiB of HBM per device.

```python
import jax
import jax.numpy as jnp
from jax import lax

BLOCK = 512
ANCS = 4
ROOTS = 8
NODES = 64


def draw_ancestors(key, part):
    indices = jnp.arange(NODES, dtype=jnp.int32)
    leading = indices % ROOTS
    columns = jnp.arange(ROOTS, dtype=jnp.int32)
    scores = jax.random.randint(key, (NODES, ROOTS), 0, 1 << 20) * ROOTS + columns[None, :]
    scores = jnp.where(columns[None, :] == leading[:, None], (1 << 20) * ROOTS + ROOTS, scores)
    ordering = jnp.argsort(scores, axis=1, stable=True).astype(jnp.int32)
    return jnp.concatenate([leading[:, None], ordering[:, :ANCS - 1]], axis=1)


def draw_parents(key, part):
    first_key, second_key = jax.random.split(jax.random.fold_in(key, 7))
    left_draw = jax.random.randint(first_key, (NODES,), 0, NODES)
    right_draw = jax.random.randint(second_key, (NODES,), 0, NODES)
    skewed = left_draw * right_draw // NODES
    indices = jnp.arange(NODES, dtype=jnp.int32)
    skewed = jnp.where(indices == 1, 0, skewed)
    return jnp.where(indices == 0, NODES - 1, skewed).astype(jnp.int32)


def block_levels(stream_key, dims, cuts, least, high):
    def one(axis_at, shards_of):
        steps = jax.random.uniform(jax.random.fold_in(jax.random.fold_in(stream_key, 6), axis_at), (shards_of,), jnp.float32, least / len(cuts), high / len(cuts))
        return jnp.repeat(jnp.exp(steps), dims[axis_at] // shards_of).reshape((-1,) + (1,) * (len(dims) - axis_at - 1))

    factor_of = one(*cuts[0])
    for cut in cuts[1:]:
        factor_of = factor_of * one(*cut)
    return factor_of


def gaussian(stream_key, dims, width, bound, pieces=(), kind=jnp.bfloat16):
    result = width * jax.random.normal(stream_key, dims, jnp.float32)
    if pieces:
        result = result * block_levels(stream_key, dims, pieces, -0.22, 0.18)
    return jnp.clip(result, -bound, bound).astype(kind)


def setup_inputs(seed: int = 0) -> dict:
    seeds = jax.random.split(jax.random.key(seed), 9)
    return {
        "root_covariance": gaussian(seeds[0], (ROOTS * BLOCK, ROOTS * BLOCK), 1.0, 6.0, ((0, 4),)),
        "ancestors": draw_ancestors(jax.random.fold_in(seeds[8], 71), 0),
        "parents": draw_parents(jax.random.fold_in(seeds[8], 71), 0),
        "panel_first": gaussian(seeds[3], (NODES, ANCS * BLOCK, BLOCK), (ANCS * BLOCK) ** -0.5, 0.125, ((0, 64), (1, 4))),
        "inverse_first": gaussian(seeds[4], (NODES, BLOCK, BLOCK), 1.0, 6.0, ((0, 64), (1, 4))),
        "panel_upper": gaussian(seeds[5], (NODES, BLOCK, BLOCK), ((ANCS + 1) * BLOCK) ** -0.5, 0.125, ((0, 64), (1, 4))),
        "panel_lower": gaussian(seeds[6], (NODES, ANCS * BLOCK, BLOCK), ((ANCS + 1) * BLOCK) ** -0.5, 0.125, ((0, 64), (1, 4))),
        "inverse_second": gaussian(seeds[7], (NODES, BLOCK, BLOCK), 1.0, 6.0, ((0, 64), (1, 4))),
    }


def select_tiles(root_covariance, chosen):
    blocks = root_covariance.reshape(ROOTS, BLOCK, ROOTS, BLOCK)
    blocks = jnp.take(jnp.take(blocks, chosen, axis=0), chosen, axis=2)
    return blocks.reshape(ANCS * BLOCK, ANCS * BLOCK)


def reference(root_covariance, ancestors, parents, panel_first, inverse_first, panel_upper, panel_lower, inverse_second):
    def first_level(items):
        chosen, panel, inverse = items
        product = jnp.dot(select_tiles(root_covariance, chosen), panel, preferred_element_type=jnp.float32)
        offdiag = (-product).astype(jnp.bfloat16)
        correction = jnp.dot(panel.T, offdiag, preferred_element_type=jnp.float32)
        diagonal = (inverse.astype(jnp.float32) - correction).astype(jnp.bfloat16)
        return offdiag, diagonal

    offdiag_first, diagonal_first = lax.map(first_level, (ancestors, panel_first, inverse_first))

    def second_level(items):
        parent, upper, lower, inverse = items
        chosen = jnp.take(ancestors, parent, axis=0)
        parent_offdiag = jnp.take(offdiag_first, parent, axis=0)
        parent_diagonal = jnp.take(diagonal_first, parent, axis=0)
        root_part = jnp.dot(select_tiles(root_covariance, chosen), lower, preferred_element_type=jnp.float32)
        lower_value = jnp.dot(parent_offdiag, upper, preferred_element_type=jnp.float32) + root_part
        upper_value = jnp.dot(parent_diagonal, upper, preferred_element_type=jnp.float32) + jnp.dot(parent_offdiag.T, lower, preferred_element_type=jnp.float32)
        offdiag_upper = (-upper_value).astype(jnp.bfloat16)
        offdiag_lower = (-lower_value).astype(jnp.bfloat16)
        correction = jnp.dot(upper.T, offdiag_upper, preferred_element_type=jnp.float32) + jnp.dot(lower.T, offdiag_lower, preferred_element_type=jnp.float32)
        diagonal = (inverse.astype(jnp.float32) - correction).astype(jnp.bfloat16)
        return offdiag_upper, offdiag_lower, diagonal

    offdiag_upper, offdiag_lower, diagonal_second = lax.map(second_level, (parents, panel_upper, panel_lower, inverse_second))
    return (offdiag_first, diagonal_first, offdiag_upper, offdiag_lower, diagonal_second)
```

```python
import jax
import jax.numpy as jnp
from jax import lax
from jax.experimental import pallas as pl
from jax.experimental.pallas import tpu as pltpu
from jax.sharding import PartitionSpec as P

BF = jnp.bfloat16
F32 = jnp.float32
VMEM_BYTES = 48 * 1024 * 1024


def vmem():
    return pl.BlockSpec(memory_space=pltpu.VMEM)


def shift(value, step):
    n = lax.axis_size("rows")
    return lax.ppermute(value, "rows", [(i, (i + step) % n) for i in range(n)])


def rows_dot(lhs, rhs):
    return lax.dot_general(lhs, rhs, (((0,), (0,)), ((), ())), preferred_element_type=F32)


def gather_rows(block):
    half = block.shape[0] // 2
    top, bottom = block[:half], block[half:]
    left_top = shift(top, 1)
    right_bottom = shift(bottom, -1)
    left_bottom = shift(bottom, 1)
    right_top = shift(top, -1)
    far_top = shift(left_top, 1)
    far_bottom = shift(right_bottom, -1)
    return (block, right_top, right_bottom, far_top, far_bottom, left_top, left_bottom)


def scatter_rows(next_two, before_two, next_a, next_b, before_a, before_b):
    from_left_two = shift(next_two, 1)
    from_right_two = shift(before_two, -1)
    left_b = shift(next_b, 1)
    right_a = shift(before_a, -1)
    left_a = shift(next_a + from_left_two, 1)
    right_b = shift(before_b + from_right_two, -1)
    return left_a, left_b, right_a, right_b


def near_kernel(ids, anc, p0, p1t, p1b, p3t, p3b, t0, t1, t3, out):
    block = pl.program_id(0)
    width = p0.shape[0]
    half = width // 2
    node, row = ids[0], ids[1]
    hits = [anc[node, lax.rem(row + d, 4)] == 2 * row + block for d in range(4)]

    @pl.when(hits[0] | hits[1] | hits[2] | hits[3])
    def _():
        total = jnp.dot(t0[...], p0[...], preferred_element_type=F32)
        for tile, top, bottom in ((t1, p1t, p1b), (t3, p3t, p3b)):
            total += jnp.dot(tile[:, :half], top[...], preferred_element_type=F32)
            total += jnp.dot(tile[:, half:], bottom[...], preferred_element_type=F32)
        out[...] = total


def first_kernel(ids, anc, p0, p1t, p1b, p2t, p2b, p3t, p3b, t2, near,
                 mine, next_a, next_b, two_a, two_b, before_a, before_b, prod, fix):
    block = pl.program_id(0)
    width = p0.shape[0]
    half = width // 2
    cut = next_a.shape[0]
    node, row = ids[0], ids[1]
    halves = ((p0.at[:half], p0.at[half:]), (p1t, p1b), (p2t, p2b), (p3t, p3b))
    targets = ((mine, None), (next_a, next_b), (two_a, two_b), (before_a, before_b))
    hits = [anc[node, lax.rem(row + d, 4)] == 2 * row + block for d in range(4)]

    @pl.when(block == 0)
    def _():
        fix[...] = jnp.zeros_like(fix)
        for a, b in targets:
            a[...] = jnp.zeros_like(a)
            if b is not None:
                b[...] = jnp.zeros_like(b)

    @pl.when(hits[0] | hits[1] | hits[2] | hits[3])
    def _():
        total = near[...]
        total += jnp.dot(t2[:, :half], p2t[...], preferred_element_type=F32)
        total += jnp.dot(t2[:, half:], p2b[...], preferred_element_type=F32)
        prod[...] = (-total).astype(BF)

    for d in range(4):
        a, b = targets[d]
        top, bottom = halves[d]

        @pl.when(hits[d])
        def _():
            if b is None:
                a[:width, :] = prod[...]
            else:
                a[...] = prod[:cut, :]
                b[: width - cut, :] = prod[cut:, :]
            fix[...] -= rows_dot(top[...], prod[:half, :]) + rows_dot(bottom[...], prod[half:, :])

    @pl.when(block == 1)
    def _():
        share = width // 4
        for d in range(4):
            start = pl.multiple_of(lax.rem(row + d, 4) * share, share)
            part = fix[pl.ds(start, share), :].astype(BF)
            a, b = targets[d]
            if b is None:
                a[width:, :] = part
            else:
                b[width - cut :, :] = part


def tile_spec(k, second):
    def index(l, ids, anc, *rest):
        node = rest[0][ids[0]] if second else ids[0]
        return l, anc[node, lax.rem(ids[1] + k, 4)]

    return pl.BlockSpec((512, 512), index)


def whole_spec(shape):
    return pl.BlockSpec(shape, lambda l, *_: (0,) * len(shape))


def near_products(ids, ancestors, pieces, root_rows):
    width = pieces[0].shape[0]
    return pl.pallas_call(
        near_kernel,
        out_shape=jax.ShapeDtypeStruct((2 * width, width), F32),
        grid_spec=pltpu.PrefetchScalarGridSpec(
            num_scalar_prefetch=2,
            grid=(2,),
            in_specs=[whole_spec(p.shape) for p in pieces]
            + [tile_spec(k, False) for k in (0, 1, 3)],
            out_specs=pl.BlockSpec((width, width), lambda l, *_: (l, 0)),
        ),
        compiler_params=pltpu.CompilerParams(vmem_limit_bytes=VMEM_BYTES),
        cost_estimate=pl.CostEstimate(
            flops=6 * width**3 * 2, bytes_accessed=6 << 20, transcendentals=0
        ),
        name="near_products",
    )(ids, ancestors, *pieces, *([root_rows] * 3))


def first_products(ids, ancestors, pieces, root_rows, near):
    width = pieces[0].shape[0]
    share = width // 4
    cut = (width + share) // 2
    shapes = [(width + share, width)] + [(cut, width)] * 6
    outs = [jax.ShapeDtypeStruct(s, BF) for s in shapes]
    return pl.pallas_call(
        first_kernel,
        out_shape=outs,
        grid_spec=pltpu.PrefetchScalarGridSpec(
            num_scalar_prefetch=2,
            grid=(2,),
            in_specs=[whole_spec(p.shape) for p in pieces]
            + [tile_spec(2, False), pl.BlockSpec((width, width), lambda l, *_: (l, 0))],
            out_specs=[whole_spec(s) for s in shapes],
            scratch_shapes=[pltpu.VMEM((width, width), BF), pltpu.VMEM((width, width), F32)],
        ),
        compiler_params=pltpu.CompilerParams(vmem_limit_bytes=VMEM_BYTES),
        cost_estimate=pl.CostEstimate(
            flops=4 * width**3 * 2, bytes_accessed=8 << 20, transcendentals=0
        ),
        name="first_products",
    )(ids, ancestors, *pieces, root_rows, near)


def second_kernel(ids, anc, parents, l0, l1, l2, l3, t0, t1, t2, t3,
                  mine, after, far, before, corr, prod):
    block = pl.program_id(0)
    row = ids[1]
    node = parents[ids[0]]
    lows = (l0, l1, l2, l3)
    outs = (mine, after, far, before)
    hits = [anc[node, lax.rem(row + d, 4)] == 2 * row + block for d in range(4)]

    @pl.when(block == 0)
    def _():
        corr[...] = jnp.zeros_like(corr)
        for out in outs:
            out[...] = jnp.zeros_like(out)

    @pl.when(hits[0] | hits[1] | hits[2] | hits[3])
    def _():
        total = None
        for tile, low in zip((t0, t1, t2, t3), lows):
            term = jnp.dot(tile[...], low[...], preferred_element_type=F32)
            total = term if total is None else total + term
        prod[...] = total.astype(BF)

    for d in range(4):

        @pl.when(hits[d])
        def _():
            outs[d][...] = prod[...]
            corr[...] += rows_dot(lows[d][...], prod[...])


def second_products(ids, ancestors, parents, lows, root_rows):
    width = lows[0].shape[1]
    square = (width, width)
    return pl.pallas_call(
        second_kernel,
        out_shape=[jax.ShapeDtypeStruct(square, BF)] * 4 + [jax.ShapeDtypeStruct(square, F32)],
        grid_spec=pltpu.PrefetchScalarGridSpec(
            num_scalar_prefetch=3,
            grid=(2,),
            in_specs=[whole_spec(square)] * 4 + [tile_spec(k, True) for k in range(4)],
            out_specs=[whole_spec(square)] * 5,
            scratch_shapes=[pltpu.VMEM(square, BF)],
        ),
        compiler_params=pltpu.CompilerParams(vmem_limit_bytes=VMEM_BYTES),
        cost_estimate=pl.CostEstimate(
            flops=6 * width**3 * 2, bytes_accessed=9 << 20, transcendentals=0
        ),
        name="second_products",
    )(ids, ancestors, parents, *lows, *([root_rows] * 4))


def settle_kernel(mine, left_a, left_b, right_a, right_b, inverse, off, diag, slices):
    width = off.shape[1]
    share = diag.shape[0]
    cut = left_a.shape[0]
    rest = width - cut
    nodes, deep, _ = slices.shape

    def total(m, x, y):
        return m.astype(F32) + x.astype(F32) + y.astype(F32)

    upper = total(mine[:cut, :], left_a[...], right_a[...])
    lower = total(mine[cut:width, :], left_b[:rest, :], right_b[:rest, :])
    off[:cut, :] = upper.astype(BF)
    off[cut:, :] = lower.astype(BF)
    value = inverse[...].astype(F32) + total(mine[width:, :], left_b[rest:, :], right_b[rest:, :])
    diag[...] = value.astype(BF)
    edge = cut // deep
    slices[:edge, :, :width] = upper.reshape(edge, deep, width).astype(BF)
    slices[edge:, :, :width] = lower.reshape(nodes - edge, deep, width).astype(BF)
    groups = share // deep
    for c in range(nodes // groups):
        part = value[:, c * 128 : (c + 1) * 128].reshape(groups, deep, 128)
        slices[c * groups : (c + 1) * groups, :, width:] = part.astype(BF)


def settle(mine, received, inverse, nodes):
    width = inverse.shape[1]
    share = inverse.shape[0]
    deep = width // nodes
    return pl.pallas_call(
        settle_kernel,
        out_shape=(
            jax.ShapeDtypeStruct((width, width), BF),
            jax.ShapeDtypeStruct((share, width), BF),
            jax.ShapeDtypeStruct((nodes, deep, width + share), BF),
        ),
        in_specs=[vmem()] * 6,
        out_specs=(vmem(),) * 3,
        compiler_params=pltpu.CompilerParams(vmem_limit_bytes=VMEM_BYTES),
        cost_estimate=pl.CostEstimate(flops=1 << 21, bytes_accessed=4 << 20, transcendentals=0),
        name="settle_first",
    )(mine, *received, inverse)


def pick_kernel(parents, held, onward):
    def step(i, carry):
        onward[i] = held[parents[i]]
        return carry

    lax.fori_loop(0, onward.shape[0], step, 0, unroll=8)


def pick(parents, held):
    return pl.pallas_call(
        pick_kernel,
        out_shape=jax.ShapeDtypeStruct(held.shape, held.dtype),
        in_specs=[pl.BlockSpec(memory_space=pltpu.SMEM), vmem()],
        out_specs=vmem(),
        compiler_params=pltpu.CompilerParams(vmem_limit_bytes=VMEM_BYTES),
        cost_estimate=pl.CostEstimate(flops=1 << 20, bytes_accessed=2 << 20, transcendentals=0),
        name="pick_parents",
    )(parents, held)


def last_kernel(ids, came, u0, u1, u2, u3, low, corr_in, off_part, keep_up, keep_diag,
                next_a, next_b, two_a, two_b, before_a, before_b, cross, corr, whole):
    nodes, deep, wide = came.shape
    width = low.shape[1]
    share = wide - width
    row = ids[1]
    for d, part in enumerate((u0, u1, u2, u3)):
        whole[lax.rem(row + d, 4)] = part[...]
    upper = whole[...].reshape(width, width)
    parent_off = came[:, :, :width].astype(F32).reshape(nodes * deep, width).astype(BF)
    groups = share // deep
    parent_diag = jnp.concatenate(
        [
            came[c * groups : (c + 1) * groups, :, width:].astype(F32).reshape(share, 128)
            for c in range(nodes // groups)
        ],
        axis=1,
    ).astype(BF)
    across = rows_dot(parent_off, low[...])
    cross[...] = across
    own = jnp.dot(parent_diag, upper, preferred_element_type=F32)
    lower = jnp.dot(parent_off, upper, preferred_element_type=F32)
    off_part[...] = lower
    corr[...] = (
        corr_in[...]
        + rows_dot(u0[...], own.astype(BF))
        + rows_dot(low[...], lower.astype(BF))
        + rows_dot(upper, across.astype(BF))
    )

    def rows_of(ref, d):
        start = pl.multiple_of(lax.rem(row + d, 4) * share, share)
        return ref[pl.ds(start, share), :]

    keep_up[...] = own + rows_of(cross, 0)
    keep_diag[...] = rows_of(corr, 0)
    for d, (a, b) in ((1, (next_a, next_b)), (2, (two_a, two_b)), (3, (before_a, before_b))):
        a[...] = rows_of(cross, d).astype(BF)
        b[...] = rows_of(corr, d).astype(BF)


def last_products(ids, came, ups, low, corr):
    width = low.shape[1]
    share = ups[0].shape[0]
    small = jax.ShapeDtypeStruct((share, width), BF)
    kept = jax.ShapeDtypeStruct((share, width), F32)
    return pl.pallas_call(
        last_kernel,
        out_shape=(jax.ShapeDtypeStruct((width, width), F32), kept, kept) + (small,) * 6,
        in_specs=[pl.BlockSpec(memory_space=pltpu.SMEM)] + [vmem()] * 7,
        out_specs=(vmem(),) * 9,
        scratch_shapes=[
            pltpu.VMEM((width, width), F32),
            pltpu.VMEM((width, width), F32),
            pltpu.VMEM((4, share, width), BF),
        ],
        compiler_params=pltpu.CompilerParams(vmem_limit_bytes=VMEM_BYTES),
        cost_estimate=pl.CostEstimate(
            flops=5 * width**3 * 2, bytes_accessed=6 << 20, transcendentals=0
        ),
        name="last_products",
    )(ids, came, *ups, low, corr)


def after(value, *others):
    return lax.optimization_barrier((value, *others))[0]


def spread_rows(block):
    return block, shift(block, -1), shift(block, 2), shift(block, 1)


def on_device(root_rows, ancestors, parents, panel_first, inverse_first, panel_upper, panel_lower,
              inverse_second):
    nodes = lax.axis_size("snode")
    ids = jnp.stack([lax.axis_index("snode"), lax.axis_index("rows")]).astype(jnp.int32)
    pieces = gather_rows(panel_first[0])
    near = near_products(ids, ancestors, pieces[:3] + pieces[5:], root_rows)
    mine, next_a, next_b, two_a, two_b, before_a, before_b = first_products(
        ids, ancestors, pieces, root_rows, near
    )
    received = scatter_rows(two_a, two_b, next_a, next_b, before_a, before_b)
    off_first, diag_first, slices = settle(mine, received, inverse_first[0], nodes)
    low, up = lax.optimization_barrier((panel_lower[0], panel_upper[0], off_first))[:2]
    lows, ups = spread_rows(low), spread_rows(up)
    spread = lax.all_to_all(slices, "snode", split_axis=0, concat_axis=0, tiled=True)
    own, to_next, to_far, to_before, corr = second_products(
        ids, ancestors, parents, lows, root_rows
    )
    picked, to_next, to_far, to_before, ups = lax.optimization_barrier(
        (pick(parents, spread), to_next, to_far, to_before, ups)
    )
    roots = (own, shift(to_next, 1), shift(to_far, 2), shift(to_before, -1))
    came = lax.all_to_all(picked, "snode", split_axis=0, concat_axis=0, tiled=True)
    off_part, keep_up, keep_diag, next_a, next_b, two_a, two_b, before_a, before_b = last_products(
        ids, came, ups, low, corr
    )
    left_a, left_b, right_a, right_b = scatter_rows(two_a, two_b, next_a, next_b, before_a, before_b)
    off_up = -(keep_up + left_a.astype(F32) + right_a.astype(F32))
    diag_second = (
        inverse_second[0].astype(F32) + keep_diag + left_b.astype(F32) + right_b.astype(F32)
    )
    off_low = off_part
    for part in roots:
        off_low = off_low + part.astype(F32)
    return (
        off_first[None],
        diag_first[None],
        off_up.astype(BF)[None],
        (-off_low).astype(BF)[None],
        diag_second.astype(BF)[None],
    )


def solution(mesh):
    split = P("snode", "rows", None)
    return jax.shard_map(
        on_device,
        mesh=mesh,
        in_specs=(P("rows", None), P(), P(), split, split, split, split, split),
        out_specs=(split,) * 5,
        check_vma=False,
    )
```

```python
import functools

import jax
import jax.numpy as jnp
from jax import lax
from jax.experimental import pallas as pl
from jax.experimental.pallas import tpu as pltpu
from jax.sharding import PartitionSpec as P

BF = jnp.bfloat16
F32 = jnp.float32
MIB = 1024 * 1024
VMEM_BYTES = 16 * MIB


def vmem():
    return pl.BlockSpec(memory_space=pltpu.VMEM)


def shift(value, step):
    n = lax.axis_size("rows")
    return lax.ppermute(value, "rows", [(i, (i + step) % n) for i in range(n)])


def rows_dot(lhs, rhs):
    return lax.dot_general(lhs, rhs, (((0,), (0,)), ((), ())), preferred_element_type=F32)


def halves_of(block):
    half = block.shape[0] // 2
    return block[:half], block[half:]


def gather_rows(block, top, bottom):
    left_top = shift(top, 1)
    right_bottom = shift(bottom, -1)
    left_bottom = shift(bottom, 1)
    right_top = shift(top, -1)
    far_top = shift(left_top, 1)
    far_bottom = shift(right_bottom, -1)
    return (block, right_top, right_bottom, far_top, far_bottom, left_top, left_bottom)


def scatter_rows(next_two, before_two, next_a, next_b, before_a, before_b):
    from_left_two = shift(next_two, 1)
    from_right_two = shift(before_two, -1)
    left_b = shift(next_b, 1)
    right_a = shift(before_a, -1)
    left_a = shift(next_a + from_left_two, 1)
    right_b = shift(before_b + from_right_two, -1)
    return left_a, left_b, right_a, right_b


def fetch(root, tiles, sems, hits, columns):
    width = tiles.shape[-1]
    copies = []
    for l in range(tiles.shape[0]):
        for k, column in enumerate(columns):
            start = pl.multiple_of(column * width, width)
            source = root.at[pl.ds(l * width, width), pl.ds(start, width)]
            copies.append(pltpu.make_async_copy(source, tiles.at[l, k], sems.at[l, k]))

    def each(l, act):
        @pl.when(hits[l])
        def _():
            for copy in copies[l * len(columns) : (l + 1) * len(columns)]:
                act(copy)

    for l in range(tiles.shape[0]):
        each(l, lambda copy: copy.start())
    return lambda l: each(l, lambda copy: copy.wait())


def hits_of(anc, node, row, block):
    return [anc[node, lax.rem(row + d, 4)] == 2 * row + block for d in range(4)]


def near_kernel(ids, anc, p0, p1t, p1b, p3t, p3b, root, out, tiles, sems):
    width = p0.shape[0]
    half = width // 2
    node, row = ids[0], ids[1]
    some = [functools.reduce(jnp.logical_or, hits_of(anc, node, row, l)) for l in range(2)]
    ready = fetch(root, tiles, sems, some, [anc[node, lax.rem(row + k, 4)] for k in (0, 1, 3)])
    for l in range(2):
        ready(l)

        @pl.when(some[l])
        def _():
            total = jnp.dot(tiles[l, 0], p0[...], preferred_element_type=F32)
            for k, top, bottom in ((1, p1t, p1b), (2, p3t, p3b)):
                total += jnp.dot(tiles[l, k, :, :half], top[...], preferred_element_type=F32)
                total += jnp.dot(tiles[l, k, :, half:], bottom[...], preferred_element_type=F32)
            out[l * width : (l + 1) * width, :] = total


def first_kernel(ids, anc, p0, p1t, p1b, p2t, p2b, p3t, p3b, near, root,
                 mine, next_a, next_b, two_a, two_b, before_a, before_b, prod, fix, tiles, sems):
    width = p0.shape[0]
    half = width // 2
    cut = next_a.shape[0]
    node, row = ids[0], ids[1]
    halves = ((p0.at[:half], p0.at[half:]), (p1t, p1b), (p2t, p2b), (p3t, p3b))
    targets = ((mine, None), (next_a, next_b), (two_a, two_b), (before_a, before_b))
    hits = [hits_of(anc, node, row, l) for l in range(2)]
    some = [functools.reduce(jnp.logical_or, h) for h in hits]
    ready = fetch(root, tiles, sems, some, [anc[node, lax.rem(row + 2, 4)]])
    fix[...] = jnp.zeros_like(fix)
    for a, b in targets:
        a[...] = jnp.zeros_like(a)
        if b is not None:
            b[...] = jnp.zeros_like(b)
    for l in range(2):
        ready(l)

        @pl.when(some[l])
        def _():
            total = near[l * width : (l + 1) * width, :]
            total += jnp.dot(tiles[l, 0, :, :half], p2t[...], preferred_element_type=F32)
            total += jnp.dot(tiles[l, 0, :, half:], p2b[...], preferred_element_type=F32)
            prod[...] = (-total).astype(BF)

        for d in range(4):
            a, b = targets[d]
            top, bottom = halves[d]

            @pl.when(hits[l][d])
            def _():
                if b is None:
                    a[:width, :] = prod[...]
                else:
                    a[...] = prod[:cut, :]
                    b[: width - cut, :] = prod[cut:, :]
                fix[...] -= rows_dot(top[...], prod[:half, :])
                fix[...] -= rows_dot(bottom[...], prod[half:, :])

    share = width // 4
    for d in range(4):
        start = pl.multiple_of(lax.rem(row + d, 4) * share, share)
        part = fix[pl.ds(start, share), :].astype(BF)
        a, b = targets[d]
        if b is None:
            a[width:, :] = part
        else:
            b[width - cut :, :] = part


def smem():
    return pl.BlockSpec(memory_space=pltpu.SMEM)


def hbm():
    return pl.BlockSpec(memory_space=pltpu.HBM)


def tile_scratch(width, count):
    return [pltpu.VMEM((2, count, width, width), BF), pltpu.SemaphoreType.DMA((2, count))]


def near_products(ids, ancestors, pieces, root_rows):
    width = pieces[0].shape[0]
    return pl.pallas_call(
        near_kernel,
        out_shape=jax.ShapeDtypeStruct((2 * width, width), F32),
        in_specs=[smem()] * 2 + [vmem()] * len(pieces) + [hbm()],
        out_specs=vmem(),
        scratch_shapes=tile_scratch(width, 3),
        compiler_params=pltpu.CompilerParams(vmem_limit_bytes=50 * MIB),
        cost_estimate=pl.CostEstimate(
            flops=6 * width**3 * 2, bytes_accessed=6 << 20, transcendentals=0
        ),
        name="near_products",
    )(ids, ancestors, *pieces, root_rows)


def first_products(ids, ancestors, pieces, root_rows, near):
    width = pieces[0].shape[0]
    share = width // 4
    cut = (width + share) // 2
    shapes = [(width + share, width)] + [(cut, width)] * 6
    return pl.pallas_call(
        first_kernel,
        out_shape=[jax.ShapeDtypeStruct(s, BF) for s in shapes],
        in_specs=[smem()] * 2 + [vmem()] * (len(pieces) + 1) + [hbm()],
        out_specs=[vmem()] * 7,
        scratch_shapes=[pltpu.VMEM((width, width), BF), pltpu.VMEM((width, width), F32)]
        + tile_scratch(width, 1),
        compiler_params=pltpu.CompilerParams(vmem_limit_bytes=VMEM_BYTES),
        cost_estimate=pl.CostEstimate(
            flops=4 * width**3 * 2, bytes_accessed=8 << 20, transcendentals=0
        ),
        name="first_products",
    )(ids, ancestors, *pieces, near, root_rows)


def second_kernel(ids, anc, parents, l0, l1, l2, l3, root,
                  mine, next_a, next_b, two_a, two_b, before_a, before_b, corr, prod, tiles, sems):
    width = l0.shape[0]
    half = width // 2
    row = ids[1]
    node = parents[ids[0]]
    lows = (l0, l1, l2, l3)
    outs = (
        (mine.at[:half], mine.at[half:]), (next_a, next_b), (two_a, two_b), (before_a, before_b)
    )
    hits = [hits_of(anc, node, row, l) for l in range(2)]
    some = [functools.reduce(jnp.logical_or, h) for h in hits]
    ready = fetch(root, tiles, sems, some, [anc[node, lax.rem(row + k, 4)] for k in range(4)])
    corr[...] = jnp.zeros_like(corr)
    for pair in outs:
        for part in pair:
            part[...] = jnp.zeros_like(part)
    for l in range(2):
        ready(l)

        @pl.when(some[l])
        def _():
            total = jnp.dot(tiles[l, 0], l0[...], preferred_element_type=F32)
            for k in range(1, 4):
                total += jnp.dot(tiles[l, k], lows[k][...], preferred_element_type=F32)
            prod[...] = total.astype(BF)

        for d in range(4):

            @pl.when(hits[l][d])
            def _():
                for k in range(2):
                    outs[d][k][...] = prod[k * half : (k + 1) * half, :]
                corr[...] += rows_dot(lows[d][...], prod[...])


def second_products(ids, ancestors, parents, lows, root_rows):
    width = lows[0].shape[1]
    square, half = (width, width), (width // 2, width)
    return pl.pallas_call(
        second_kernel,
        out_shape=[jax.ShapeDtypeStruct(square, BF)]
        + [jax.ShapeDtypeStruct(half, BF)] * 6
        + [jax.ShapeDtypeStruct(square, F32)],
        in_specs=[smem()] * 3 + [vmem()] * 4 + [hbm()],
        out_specs=[vmem()] * 8,
        scratch_shapes=[pltpu.VMEM(square, BF)] + tile_scratch(width, 4),
        compiler_params=pltpu.CompilerParams(vmem_limit_bytes=46 * MIB),
        cost_estimate=pl.CostEstimate(
            flops=30 * width**3 * 2, bytes_accessed=9 << 20, transcendentals=0
        ),
        name="second_products",
    )(ids, ancestors, parents, *lows, root_rows)


def settle_kernel(mine, left_a, left_b, right_a, right_b, inverse, off, diag, slices):
    width = off.shape[1]
    share = diag.shape[0]
    cut = left_a.shape[0]
    rest = width - cut
    nodes, deep, _ = slices.shape

    def total(m, x, y):
        return m.astype(F32) + x.astype(F32) + y.astype(F32)

    upper = total(mine[:cut, :], left_a[...], right_a[...])
    lower = total(mine[cut:width, :], left_b[:rest, :], right_b[:rest, :])
    off[:cut, :] = upper.astype(BF)
    off[cut:, :] = lower.astype(BF)
    value = inverse[...].astype(F32) + total(mine[width:, :], left_b[rest:, :], right_b[rest:, :])
    diag[...] = value.astype(BF)
    edge = cut // deep
    slices[:edge, :, :width] = upper.reshape(edge, deep, width).astype(BF)
    slices[edge:, :, :width] = lower.reshape(nodes - edge, deep, width).astype(BF)
    groups = share // deep
    for c in range(nodes // groups):
        part = value[:, c * 128 : (c + 1) * 128].reshape(groups, deep, 128)
        slices[c * groups : (c + 1) * groups, :, width:] = part.astype(BF)


def settle(mine, received, inverse, nodes):
    width = inverse.shape[1]
    share = inverse.shape[0]
    deep = width // nodes
    return pl.pallas_call(
        settle_kernel,
        out_shape=(
            jax.ShapeDtypeStruct((width, width), BF),
            jax.ShapeDtypeStruct((share, width), BF),
            jax.ShapeDtypeStruct((nodes, deep, width + share), BF),
        ),
        in_specs=[vmem()] * 6,
        out_specs=(vmem(),) * 3,
        compiler_params=pltpu.CompilerParams(vmem_limit_bytes=VMEM_BYTES),
        cost_estimate=pl.CostEstimate(flops=1 << 21, bytes_accessed=4 << 20, transcendentals=0),
        name="settle_first",
    )(mine, *received, inverse)


def pick_kernel(parents, held, onward):
    def step(i, carry):
        onward[i] = held[parents[i]]
        return carry

    lax.fori_loop(0, onward.shape[0], step, 0, unroll=8)


def pick(parents, held):
    return pl.pallas_call(
        pick_kernel,
        out_shape=jax.ShapeDtypeStruct(held.shape, held.dtype),
        in_specs=[pl.BlockSpec(memory_space=pltpu.SMEM), vmem()],
        out_specs=vmem(),
        compiler_params=pltpu.CompilerParams(vmem_limit_bytes=VMEM_BYTES),
        cost_estimate=pl.CostEstimate(flops=1 << 20, bytes_accessed=2 << 20, transcendentals=0),
        name="pick_parents",
    )(parents, held)


def sum_kernel(own, left_a, left_b, right_a, right_b, out):
    half = left_a.shape[0]
    for rows, left, right in ((slice(0, half), left_a, right_a), (slice(half, None), left_b, right_b)):
        out[rows, :] = own[rows, :].astype(F32) + left[...].astype(F32) + right[...].astype(F32)


def sum_roots(own, received):
    shape = own.shape
    return pl.pallas_call(
        sum_kernel,
        out_shape=jax.ShapeDtypeStruct(shape, F32),
        in_specs=[vmem()] * 5,
        out_specs=vmem(),
        compiler_params=pltpu.CompilerParams(vmem_limit_bytes=VMEM_BYTES),
        cost_estimate=pl.CostEstimate(
            flops=48 * shape[0] ** 3 * 2, bytes_accessed=3 << 20, transcendentals=0
        ),
        name="sum_roots",
    )(own, *received)


def last_kernel(ids, came, u0, u1, u2, u3, low, corr_in, root, off_low, keep_up, keep_diag,
                next_a, next_b, two_a, two_b, before_a, before_b, cross, corr, whole):
    nodes, deep, wide = came.shape
    width = low.shape[1]
    share = wide - width
    row = ids[1]
    for d, part in enumerate((u0, u1, u2, u3)):
        whole[lax.rem(row + d, 4)] = part[...]
    upper = whole[...].reshape(width, width)
    parent_off = came[:, :, :width].astype(F32).reshape(nodes * deep, width).astype(BF)
    groups = share // deep
    parent_diag = jnp.concatenate(
        [
            came[c * groups : (c + 1) * groups, :, width:].astype(F32).reshape(share, 128)
            for c in range(nodes // groups)
        ],
        axis=1,
    ).astype(BF)
    across = rows_dot(parent_off, low[...])
    cross[...] = across
    own = jnp.dot(parent_diag, upper, preferred_element_type=F32)
    lower = jnp.dot(parent_off, upper, preferred_element_type=F32)
    off_low[...] = -(lower + root[...]).astype(BF)
    corr[...] = (
        corr_in[...]
        + rows_dot(u0[...], own.astype(BF))
        + rows_dot(low[...], lower.astype(BF))
        + rows_dot(upper, across.astype(BF))
    )

    def rows_of(ref, d):
        start = pl.multiple_of(lax.rem(row + d, 4) * share, share)
        return ref[pl.ds(start, share), :]

    keep_up[...] = own + rows_of(cross, 0)
    keep_diag[...] = rows_of(corr, 0)
    for d, (a, b) in ((1, (next_a, next_b)), (2, (two_a, two_b)), (3, (before_a, before_b))):
        a[...] = rows_of(cross, d).astype(BF)
        b[...] = rows_of(corr, d).astype(BF)


def last_products(ids, came, ups, low, corr, root):
    width = low.shape[1]
    share = ups[0].shape[0]
    small = jax.ShapeDtypeStruct((share, width), BF)
    kept = jax.ShapeDtypeStruct((share, width), F32)
    return pl.pallas_call(
        last_kernel,
        out_shape=(jax.ShapeDtypeStruct((width, width), BF), kept, kept) + (small,) * 6,
        in_specs=[pl.BlockSpec(memory_space=pltpu.SMEM)] + [vmem()] * 8,
        out_specs=(vmem(),) * 9,
        scratch_shapes=[
            pltpu.VMEM((width, width), F32),
            pltpu.VMEM((width, width), F32),
            pltpu.VMEM((4, share, width), BF),
        ],
        compiler_params=pltpu.CompilerParams(vmem_limit_bytes=VMEM_BYTES),
        cost_estimate=pl.CostEstimate(
            flops=5 * width**3 * 2, bytes_accessed=6 << 20, transcendentals=0
        ),
        name="last_products",
    )(ids, came, *ups, low, corr, root)


def after(value, *others):
    return lax.optimization_barrier((value, *others))[0]


def spread_rows(block):
    return block, shift(block, -1), shift(block, 2), shift(block, 1)


def on_device(root_rows, ancestors, parents, panel_first, inverse_first, panel_upper, panel_lower,
              inverse_second):
    nodes = lax.axis_size("snode")
    ids = jnp.stack([lax.axis_index("snode"), lax.axis_index("rows")]).astype(jnp.int32)
    pieces = gather_rows(panel_first[0], *halves_of(panel_first[0]))
    near = near_products(ids, ancestors, pieces[:3] + pieces[5:], root_rows)
    mine, next_a, next_b, two_a, two_b, before_a, before_b = first_products(
        ids, ancestors, pieces, root_rows, near
    )
    received = scatter_rows(two_a, two_b, next_a, next_b, before_a, before_b)
    off_first, diag_first, slices = settle(mine, received, inverse_first[0], nodes)
    low = panel_lower[0]
    sent, up = lax.optimization_barrier((low, panel_upper[0], off_first))[:2]
    lows, ups = spread_rows(sent), spread_rows(up)
    spread = lax.all_to_all(slices, "snode", split_axis=0, concat_axis=0, tiled=True)
    own, next_a, next_b, two_a, two_b, before_a, before_b, corr = second_products(
        ids, ancestors, parents, lows, root_rows
    )
    picked, ups = lax.optimization_barrier((pick(parents, spread), ups))
    received = scatter_rows(two_a, two_b, next_a, next_b, before_a, before_b)
    came = lax.all_to_all(picked, "snode", split_axis=0, concat_axis=0, tiled=True)
    off_low, keep_up, keep_diag, next_a, next_b, two_a, two_b, before_a, before_b = last_products(
        ids, came, ups, low, corr, sum_roots(own, received)
    )
    left_a, left_b, right_a, right_b = scatter_rows(two_a, two_b, next_a, next_b, before_a, before_b)
    off_up = -(keep_up + left_a.astype(F32) + right_a.astype(F32))
    diag_second = (
        inverse_second[0].astype(F32) + keep_diag + left_b.astype(F32) + right_b.astype(F32)
    )
    return (
        off_first[None],
        diag_first[None],
        off_up.astype(BF)[None],
        off_low[None],
        diag_second.astype(BF)[None],
    )


def solution(mesh):
    split = P("snode", "rows", None)
    return jax.shard_map(
        on_device,
        mesh=mesh,
        in_specs=(P("rows", None), P(), P(), split, split, split, split, split),
        out_specs=(split,) * 5,
        check_vma=False,
    )
```

```python
import functools

import jax
import jax.numpy as jnp
from jax import lax
from jax.experimental import pallas as pl
from jax.experimental.pallas import tpu as pltpu
from jax.sharding import PartitionSpec as P

BF = jnp.bfloat16
F32 = jnp.float32
MIB = 1024 * 1024
VMEM_BYTES = 16 * MIB


def vmem():
    return pl.BlockSpec(memory_space=pltpu.VMEM)


def shift(value, step):
    n = lax.axis_size("rows")
    return lax.ppermute(value, "rows", [(i, (i + step) % n) for i in range(n)])


def rows_dot(lhs, rhs):
    return lax.dot_general(lhs, rhs, (((0,), (0,)), ((), ())), preferred_element_type=F32)


def halves_of(block):
    half = block.shape[0] // 2
    return block[:half], block[half:]


def gather_rows(block, top, bottom):
    left_top = shift(top, 1)
    right_bottom = shift(bottom, -1)
    left_bottom = shift(bottom, 1)
    right_top = shift(top, -1)
    far_top = shift(left_top, 1)
    far_bottom = shift(right_bottom, -1)
    return (block, right_top, right_bottom, far_top, far_bottom, left_top, left_bottom)


def scatter_rows(next_two, before_two, next_a, next_b, before_a, before_b):
    from_left_two = shift(next_two, 1)
    from_right_two = shift(before_two, -1)
    left_b = shift(next_b, 1)
    right_a = shift(before_a, -1)
    left_a = shift(next_a + from_left_two, 1)
    right_b = shift(before_b + from_right_two, -1)
    return left_a, left_b, right_a, right_b


def fetch(root, tiles, sems, hits, columns):
    width = tiles.shape[-1]
    copies = []
    for l in range(tiles.shape[0]):
        for k, column in enumerate(columns):
            start = pl.multiple_of(column * width, width)
            source = root.at[pl.ds(l * width, width), pl.ds(start, width)]
            copies.append(pltpu.make_async_copy(source, tiles.at[l, k], sems.at[l, k]))

    def each(l, act):
        @pl.when(hits[l])
        def _():
            for copy in copies[l * len(columns) : (l + 1) * len(columns)]:
                act(copy)

    for l in range(tiles.shape[0]):
        each(l, lambda copy: copy.start())
    return lambda l: each(l, lambda copy: copy.wait())


def hits_of(anc, node, row, block):
    return [anc[node, lax.rem(row + d, 4)] == 2 * row + block for d in range(4)]


def near_kernel(ids, anc, p0, p1t, p1b, p3t, p3b, root, out, tiles, sems):
    width = p0.shape[0]
    half = width // 2
    node, row = ids[0], ids[1]
    some = [functools.reduce(jnp.logical_or, hits_of(anc, node, row, l)) for l in range(2)]
    ready = fetch(root, tiles, sems, some, [anc[node, lax.rem(row + k, 4)] for k in (0, 1, 3)])
    for l in range(2):
        ready(l)

        @pl.when(some[l])
        def _():
            total = jnp.dot(tiles[l, 0], p0[...], preferred_element_type=F32)
            for k, top, bottom in ((1, p1t, p1b), (2, p3t, p3b)):
                total += jnp.dot(tiles[l, k, :, :half], top[...], preferred_element_type=F32)
                total += jnp.dot(tiles[l, k, :, half:], bottom[...], preferred_element_type=F32)
            out[l * width : (l + 1) * width, :] = total


def first_kernel(ids, anc, p0, p1t, p1b, p2t, p2b, p3t, p3b, near, root,
                 mine, next_a, next_b, two_a, two_b, before_a, before_b, prod, fix, tiles, sems):
    width = p0.shape[0]
    half = width // 2
    cut = next_a.shape[0]
    node, row = ids[0], ids[1]
    halves = ((p0.at[:half], p0.at[half:]), (p1t, p1b), (p2t, p2b), (p3t, p3b))
    targets = ((mine, None), (next_a, next_b), (two_a, two_b), (before_a, before_b))
    hits = [hits_of(anc, node, row, l) for l in range(2)]
    some = [functools.reduce(jnp.logical_or, h) for h in hits]
    ready = fetch(root, tiles, sems, some, [anc[node, lax.rem(row + 2, 4)]])
    fix[...] = jnp.zeros_like(fix)
    for a, b in targets:
        a[...] = jnp.zeros_like(a)
        if b is not None:
            b[...] = jnp.zeros_like(b)
    for l in range(2):
        ready(l)

        @pl.when(some[l])
        def _():
            total = near[l * width : (l + 1) * width, :]
            total += jnp.dot(tiles[l, 0, :, :half], p2t[...], preferred_element_type=F32)
            total += jnp.dot(tiles[l, 0, :, half:], p2b[...], preferred_element_type=F32)
            prod[...] = (-total).astype(BF)

        for d in range(4):
            a, b = targets[d]
            top, bottom = halves[d]

            @pl.when(hits[l][d])
            def _():
                if b is None:
                    a[:width, :] = prod[...]
                else:
                    a[...] = prod[:cut, :]
                    b[: width - cut, :] = prod[cut:, :]
                fix[...] -= rows_dot(top[...], prod[:half, :])
                fix[...] -= rows_dot(bottom[...], prod[half:, :])

    share = width // 4
    for d in range(4):
        start = pl.multiple_of(lax.rem(row + d, 4) * share, share)
        part = fix[pl.ds(start, share), :].astype(BF)
        a, b = targets[d]
        if b is None:
            a[width:, :] = part
        else:
            b[width - cut :, :] = part


def smem():
    return pl.BlockSpec(memory_space=pltpu.SMEM)


def hbm():
    return pl.BlockSpec(memory_space=pltpu.HBM)


def tile_scratch(width, count):
    return [pltpu.VMEM((2, count, width, width), BF), pltpu.SemaphoreType.DMA((2, count))]


def near_products(ids, ancestors, pieces, root_rows):
    width = pieces[0].shape[0]
    return pl.pallas_call(
        near_kernel,
        out_shape=jax.ShapeDtypeStruct((2 * width, width), F32),
        in_specs=[smem()] * 2 + [vmem()] * len(pieces) + [hbm()],
        out_specs=vmem(),
        scratch_shapes=tile_scratch(width, 3),
        compiler_params=pltpu.CompilerParams(vmem_limit_bytes=50 * MIB),
        cost_estimate=pl.CostEstimate(
            flops=6 * width**3 * 2, bytes_accessed=6 << 20, transcendentals=0
        ),
        name="near_products",
    )(ids, ancestors, *pieces, root_rows)


def first_products(ids, ancestors, pieces, root_rows, near):
    width = pieces[0].shape[0]
    share = width // 4
    cut = (width + share) // 2
    shapes = [(width + share, width)] + [(cut, width)] * 6
    return pl.pallas_call(
        first_kernel,
        out_shape=[jax.ShapeDtypeStruct(s, BF) for s in shapes],
        in_specs=[smem()] * 2 + [vmem()] * (len(pieces) + 1) + [hbm()],
        out_specs=[vmem()] * 7,
        scratch_shapes=[pltpu.VMEM((width, width), BF), pltpu.VMEM((width, width), F32)]
        + tile_scratch(width, 1),
        compiler_params=pltpu.CompilerParams(vmem_limit_bytes=VMEM_BYTES),
        cost_estimate=pl.CostEstimate(
            flops=4 * width**3 * 2, bytes_accessed=8 << 20, transcendentals=0
        ),
        name="first_products",
    )(ids, ancestors, *pieces, near, root_rows)


def second_kernel(ids, anc, parents, l0, l1, l2, l3, root,
                  mine, next_a, next_b, two_a, two_b, before_a, before_b, corr, prod, tiles, sems):
    width = l0.shape[0]
    half = width // 2
    row = ids[1]
    node = parents[ids[0]]
    lows = (l0, l1, l2, l3)
    outs = (
        (mine.at[:half], mine.at[half:]), (next_a, next_b), (two_a, two_b), (before_a, before_b)
    )
    hits = [hits_of(anc, node, row, l) for l in range(2)]
    some = [functools.reduce(jnp.logical_or, h) for h in hits]
    ready = fetch(root, tiles, sems, some, [anc[node, lax.rem(row + k, 4)] for k in range(4)])
    corr[...] = jnp.zeros_like(corr)
    for pair in outs:
        for part in pair:
            part[...] = jnp.zeros_like(part)
    for l in range(2):
        ready(l)

        @pl.when(some[l])
        def _():
            total = jnp.dot(tiles[l, 0], l0[...], preferred_element_type=F32)
            for k in range(1, 4):
                total += jnp.dot(tiles[l, k], lows[k][...], preferred_element_type=F32)
            prod[...] = total.astype(BF)

        for d in range(4):

            @pl.when(hits[l][d])
            def _():
                for k in range(2):
                    outs[d][k][...] = prod[k * half : (k + 1) * half, :]
                corr[...] += rows_dot(lows[d][...], prod[...])


def second_products(ids, ancestors, parents, lows, root_rows):
    width = lows[0].shape[1]
    square, half = (width, width), (width // 2, width)
    return pl.pallas_call(
        second_kernel,
        out_shape=[jax.ShapeDtypeStruct(square, BF)]
        + [jax.ShapeDtypeStruct(half, BF)] * 6
        + [jax.ShapeDtypeStruct(square, F32)],
        in_specs=[smem()] * 3 + [vmem()] * 4 + [hbm()],
        out_specs=[vmem()] * 8,
        scratch_shapes=[pltpu.VMEM(square, BF)] + tile_scratch(width, 4),
        compiler_params=pltpu.CompilerParams(vmem_limit_bytes=46 * MIB),
        cost_estimate=pl.CostEstimate(
            flops=40 * width**3 * 2, bytes_accessed=9 << 20, transcendentals=0
        ),
        name="second_products",
    )(ids, ancestors, parents, *lows, root_rows)


def settle_kernel(mine, left_a, left_b, right_a, right_b, inverse, off, diag, slices):
    width = off.shape[1]
    share = diag.shape[0]
    cut = left_a.shape[0]
    rest = width - cut
    nodes, deep, _ = slices.shape

    def total(m, x, y):
        return m.astype(F32) + x.astype(F32) + y.astype(F32)

    upper = total(mine[:cut, :], left_a[...], right_a[...])
    lower = total(mine[cut:width, :], left_b[:rest, :], right_b[:rest, :])
    off[:cut, :] = upper.astype(BF)
    off[cut:, :] = lower.astype(BF)
    value = inverse[...].astype(F32) + total(mine[width:, :], left_b[rest:, :], right_b[rest:, :])
    diag[...] = value.astype(BF)
    edge = cut // deep
    slices[:edge, :, :width] = upper.reshape(edge, deep, width).astype(BF)
    slices[edge:, :, :width] = lower.reshape(nodes - edge, deep, width).astype(BF)
    groups = share // deep
    for c in range(nodes // groups):
        part = value[:, c * 128 : (c + 1) * 128].reshape(groups, deep, 128)
        slices[c * groups : (c + 1) * groups, :, width:] = part.astype(BF)


def settle(mine, received, inverse, nodes):
    width = inverse.shape[1]
    share = inverse.shape[0]
    deep = width // nodes
    return pl.pallas_call(
        settle_kernel,
        out_shape=(
            jax.ShapeDtypeStruct((width, width), BF),
            jax.ShapeDtypeStruct((share, width), BF),
            jax.ShapeDtypeStruct((nodes, deep, width + share), BF),
        ),
        in_specs=[vmem()] * 6,
        out_specs=(vmem(),) * 3,
        compiler_params=pltpu.CompilerParams(vmem_limit_bytes=VMEM_BYTES),
        cost_estimate=pl.CostEstimate(flops=1 << 21, bytes_accessed=4 << 20, transcendentals=0),
        name="settle_first",
    )(mine, *received, inverse)


def pick_kernel(parents, held, onward):
    def step(i, carry):
        onward[i] = held[parents[i]]
        return carry

    lax.fori_loop(0, onward.shape[0], step, 0, unroll=8)


def pick(parents, held):
    return pl.pallas_call(
        pick_kernel,
        out_shape=jax.ShapeDtypeStruct(held.shape, held.dtype),
        in_specs=[pl.BlockSpec(memory_space=pltpu.SMEM), vmem()],
        out_specs=vmem(),
        compiler_params=pltpu.CompilerParams(vmem_limit_bytes=VMEM_BYTES),
        cost_estimate=pl.CostEstimate(flops=1 << 20, bytes_accessed=2 << 20, transcendentals=0),
        name="pick_parents",
    )(parents, held)


def sum_kernel(own, left_a, left_b, right_a, right_b, out):
    half = left_a.shape[0]
    for rows, left, right in ((slice(0, half), left_a, right_a), (slice(half, None), left_b, right_b)):
        total = own[rows, :].astype(F32) + left[...].astype(F32) + right[...].astype(F32)
        out[rows, :] = total.astype(BF)


def sum_roots(own, received):
    shape = own.shape
    return pl.pallas_call(
        sum_kernel,
        out_shape=jax.ShapeDtypeStruct(shape, BF),
        in_specs=[vmem()] * 5,
        out_specs=vmem(),
        compiler_params=pltpu.CompilerParams(vmem_limit_bytes=VMEM_BYTES),
        cost_estimate=pl.CostEstimate(
            flops=40 * shape[0] ** 3 * 2, bytes_accessed=3 << 20, transcendentals=0
        ),
        name="sum_roots",
    )(own, *received)


def last_kernel(ids, came, u0, u1, u2, u3, low, corr_in, root, off_low, keep_up, keep_diag,
                next_a, next_b, two_a, two_b, before_a, before_b, cross, corr, whole):
    nodes, deep, wide = came.shape
    width = low.shape[1]
    share = wide - width
    row = ids[1]
    for d, part in enumerate((u0, u1, u2, u3)):
        whole[lax.rem(row + d, 4)] = part[...]
    upper = whole[...].reshape(width, width)
    parent_off = came[:, :, :width].astype(F32).reshape(nodes * deep, width).astype(BF)
    groups = share // deep
    parent_diag = jnp.concatenate(
        [
            came[c * groups : (c + 1) * groups, :, width:].astype(F32).reshape(share, 128)
            for c in range(nodes // groups)
        ],
        axis=1,
    ).astype(BF)
    across = rows_dot(parent_off, low[...])
    cross[...] = across
    own = jnp.dot(parent_diag, upper, preferred_element_type=F32)
    lower = jnp.dot(parent_off, upper, preferred_element_type=F32)
    off_low[...] = -(lower + root[...].astype(F32)).astype(BF)
    corr[...] = (
        corr_in[...]
        + rows_dot(u0[...], own.astype(BF))
        + rows_dot(low[...], lower.astype(BF))
        + rows_dot(upper, across.astype(BF))
    )

    def rows_of(ref, d):
        start = pl.multiple_of(lax.rem(row + d, 4) * share, share)
        return ref[pl.ds(start, share), :]

    keep_up[...] = own + rows_of(cross, 0)
    keep_diag[...] = rows_of(corr, 0)
    for d, (a, b) in ((1, (next_a, next_b)), (2, (two_a, two_b)), (3, (before_a, before_b))):
        a[...] = rows_of(cross, d).astype(BF)
        b[...] = rows_of(corr, d).astype(BF)


def last_products(ids, came, ups, low, corr, root):
    width = low.shape[1]
    share = ups[0].shape[0]
    small = jax.ShapeDtypeStruct((share, width), BF)
    kept = jax.ShapeDtypeStruct((share, width), F32)
    return pl.pallas_call(
        last_kernel,
        out_shape=(jax.ShapeDtypeStruct((width, width), BF), kept, kept) + (small,) * 6,
        in_specs=[pl.BlockSpec(memory_space=pltpu.SMEM)] + [vmem()] * 8,
        out_specs=(vmem(),) * 9,
        scratch_shapes=[
            pltpu.VMEM((width, width), F32),
            pltpu.VMEM((width, width), F32),
            pltpu.VMEM((4, share, width), BF),
        ],
        compiler_params=pltpu.CompilerParams(vmem_limit_bytes=VMEM_BYTES),
        cost_estimate=pl.CostEstimate(
            flops=5 * width**3 * 2, bytes_accessed=6 << 20, transcendentals=0
        ),
        name="last_products",
    )(ids, came, *ups, low, corr, root)


def after(value, *others):
    return lax.optimization_barrier((value, *others))[0]


def spread_rows(block):
    return block, shift(block, -1), shift(block, 2), shift(block, 1)


def on_device(root_rows, ancestors, parents, panel_first, inverse_first, panel_upper, panel_lower,
              inverse_second):
    nodes = lax.axis_size("snode")
    ids = jnp.stack([lax.axis_index("snode"), lax.axis_index("rows")]).astype(jnp.int32)
    pieces = gather_rows(panel_first[0], *halves_of(panel_first[0]))
    near = near_products(ids, ancestors, pieces[:3] + pieces[5:], root_rows)
    mine, next_a, next_b, two_a, two_b, before_a, before_b = first_products(
        ids, ancestors, pieces, root_rows, near
    )
    received = scatter_rows(two_a, two_b, next_a, next_b, before_a, before_b)
    off_first, diag_first, slices = settle(mine, received, inverse_first[0], nodes)
    low = panel_lower[0]
    sent, up = lax.optimization_barrier((low, panel_upper[0], *received[1:3]))[:2]
    lows, ups = spread_rows(sent), spread_rows(up)
    spread = lax.all_to_all(slices, "snode", split_axis=0, concat_axis=0, tiled=True)
    own, next_a, next_b, two_a, two_b, before_a, before_b, corr = second_products(
        ids, ancestors, parents, lows, root_rows
    )
    picked, next_a, next_b, two_a, two_b, before_a, before_b, ups = lax.optimization_barrier(
        (pick(parents, spread), next_a, next_b, two_a, two_b, before_a, before_b, ups)
    )
    received = scatter_rows(two_a, two_b, next_a, next_b, before_a, before_b)
    came = lax.all_to_all(picked, "snode", split_axis=0, concat_axis=0, tiled=True)
    off_low, keep_up, keep_diag, next_a, next_b, two_a, two_b, before_a, before_b = last_products(
        ids, came, ups, low, corr, sum_roots(own, received)
    )
    left_a, left_b, right_a, right_b = scatter_rows(two_a, two_b, next_a, next_b, before_a, before_b)
    off_up = -(keep_up + left_a.astype(F32) + right_a.astype(F32))
    diag_second = (
        inverse_second[0].astype(F32) + keep_diag + left_b.astype(F32) + right_b.astype(F32)
    )
    return (
        off_first[None],
        diag_first[None],
        off_up.astype(BF)[None],
        off_low[None],
        diag_second.astype(BF)[None],
    )


def solution(mesh):
    split = P("snode", "rows", None)
    return jax.shard_map(
        on_device,
        mesh=mesh,
        in_specs=(P("rows", None), P(), P(), split, split, split, split, split),
        out_specs=(split,) * 5,
        check_vma=False,
    )
```
